32 devices in a mesh: groups: 2 (over x), owner: 8 (over z, y), tile: 2 (over core).
Axes of the slice: x: 2, y: 2, z: 4, core: 2. Of those that a mesh axis runs over, the one named last changes fastest.
Arguments:
- embeddings: bfloat16 [32768, 768], P(('groups', 'owner', 'tile')), parts along dimension 0, may hold values from -8 to 8
- cluster_ids: int32 [32768], P(('groups', 'owner', 'tile')), parts along dimension 0, may hold values from 0 to 15, as said below
Outputs:
- dup_score: float32 [32768], P(('groups', 'owner', 'tile')), parts along dimension 0
The draws below stay inside these ranges and needn't reach their ends.
There are 2 independent parts, one for each index of `groups`. The reference program is written for one: setup_inputs(seed, part) draws one part's arguments, and reference() takes and returns one part's arrays. A program takes and returns all parts, laid end to end along the dimension named above; each array names one. Nothing has to cross between parts.
Inputs may be any that keep to these rules, and one draw needn't show every extreme that they name: `cluster_ids`: in each aligned block of 1024 rows (the rows of one device) no cluster is named more than 128 times; some cluster is named exactly 128 times in every block.
All inputs are finite; a program needn't handle non-finite values.
Results may differ from the reference program's by a relative error of at most 0.0045.
Values may be sent and summed in bfloat16 or wider, within the bound.
A program may use at most 64 MiB of HBM per device.

```python
import jax
import jax.numpy as jnp
from jax import lax

D = 768
ROWS_DEV = 1024
CLUS_OWN = 2
CLUSTERS = 16
CAP = 128
ROWS = 16384
N_OWNER = 8
N_TILE = 2


def slot_rows(key):
    devices = N_OWNER * N_TILE
    slots = CLUSTERS * CAP
    keys = jax.random.split(key, 5)
    weight = jax.random.randint(keys[0], (CLUSTERS,), 0, 8)
    noise = jax.random.randint(keys[1], (devices, slots), 0, 4096)
    shared = jax.random.randint(keys[2], (), 0, CLUSTERS)
    own_full = jax.random.randint(keys[3], (devices,), 0, CLUSTERS)
    cluster_of = jnp.arange(slots, dtype=jnp.int32) // CAP
    forced = ((cluster_of[None, :] == shared) | (cluster_of[None, :] == own_full[:, None])).astype(jnp.int32)
    score = noise + weight[cluster_of][None, :] * 512 + forced * 8192
    distinct = score * slots + jnp.arange(slots, dtype=jnp.int32)[None, :]
    chosen = lax.top_k(distinct, ROWS_DEV)[1].astype(jnp.int32)
    order_key = jax.random.randint(keys[4], (devices, ROWS_DEV), 0, 65536) * ROWS_DEV + jnp.arange(ROWS_DEV, dtype=jnp.int32)[None, :]
    order = lax.top_k(order_key, ROWS_DEV)[1]
    chosen = jnp.take_along_axis(chosen, order, axis=1)
    return chosen.reshape(-1).astype(jnp.int32)


def draw_cluster_ids(key, part):
    chosen = slot_rows(key)
    return (chosen // CAP).astype(jnp.int32)


def draw_embeddings(key, part):
    chosen = slot_rows(key)
    key = jax.random.fold_in(key, 7)
    keys = jax.random.split(key, 5)
    cluster = chosen // CAP
    topic = chosen // 4
    topic_count = (CLUSTERS * CAP + 3) // 4
    centers = jax.random.truncated_normal(keys[0], -4.0, 4.0, (CLUSTERS, D), jnp.float32)
    mix = jax.random.uniform(keys[1], (CLUSTERS,), jnp.float32, 0.6, 0.72)
    topics = jax.random.truncated_normal(keys[2], -4.0, 4.0, (topic_count, D), jnp.float32)
    twins = jax.random.truncated_normal(keys[3], -4.0, 4.0, (CLUSTERS * CAP, D), jnp.float32)
    alpha = jnp.sqrt(mix[cluster])[:, None]
    delta = jnp.sqrt(1.0 - mix[cluster] - 0.22)[:, None]
    rough = jax.random.truncated_normal(keys[4], -4.0, 4.0, (ROWS, D), jnp.float32)
    scale = 2.0 * jnp.ones((ROWS, 1), jnp.float32)
    shape_part = alpha * centers[cluster] + 0.31622777 * topics[topic] + 0.34641016 * twins[chosen] + delta * rough
    values = scale * shape_part
    return jnp.clip(values, -8.0, 8.0).astype(jnp.bfloat16)


def setup_inputs(seed: int = 0, part: int = 0) -> dict:
    seeds = jax.random.split(jax.random.key(seed), 3)
    part_splits = jax.random.split(jax.random.fold_in(seeds[2], part), 3)
    return {
        "embeddings": draw_embeddings(jax.random.fold_in(jax.random.fold_in(seeds[2], part), 71), part),
        "cluster_ids": draw_cluster_ids(jax.random.fold_in(jax.random.fold_in(seeds[2], part), 71), part),
    }


epsilon = 1e-06
sharpness = 20.0

def reference(embeddings, cluster_ids):
    values = embeddings.astype(jnp.float32)
    scale = lax.rsqrt(lax.optimization_barrier(jnp.sum(values * values, axis=1, keepdims=True)) + epsilon)
    unit = (values * scale).astype(jnp.bfloat16)
    members = N_OWNER * N_TILE * CAP
    clusters = CLUS_OWN * N_OWNER

    def one_cluster(cluster):
        inside = cluster_ids == cluster
        count = jnp.sum(inside.astype(jnp.int32))
        where_rows = jnp.nonzero(inside, size=members, fill_value=0)[0].astype(jnp.int32)
        live = (jnp.arange(members, dtype=jnp.int32) < count).astype(jnp.float32)
        picked = unit[where_rows].astype(jnp.float32)
        cosine = jnp.dot(picked, picked.T, precision=lax.Precision.HIGHEST)
        kernel = jnp.exp(sharpness * (cosine - 1.0)) * live[None, :]
        return (lax.optimization_barrier(jnp.sum(kernel, axis=1)) * live, where_rows)
    sums, where_all = lax.map(one_cluster, jnp.arange(clusters, dtype=jnp.int32))
    score = jnp.zeros((embeddings.shape[0],), jnp.float32).at[where_all.reshape(-1)].add(sums.reshape(-1))
    return jnp.log(score)
```

```python
import functools

import jax
import jax.numpy as jnp
from jax import lax
from jax.experimental import pallas as pl
from jax.experimental.pallas import tpu as pltpu
from jax.sharding import PartitionSpec as P

CLUS_OWN = 2
LANES = 128
MESH = pl.DeviceIdType.MESH

epsilon = 1e-06
sharpness = 20.0


def flipped(index, offset, count):
    total = 0
    bit = 1
    while bit < count:
        digit = lax.rem(lax.div(index, bit) + lax.div(offset, bit), 2)
        total = total + digit * bit
        bit *= 2
    return total


def fold(values):
    rows, lanes = values.shape
    return jnp.sum(values.reshape(rows // 8, 8, lanes), axis=0)


def dup_kernel(
    n, cap, x_ref, id_ref, out_ref,
    unit, within_ref, chosen, outgoing, held, count_out, count_in, sums,
    score_out, score_in, spread,
    send_sem, recv_sem, csend_sem, crecv_sem,
    fsend_sem, frecv_sem, fcsend_sem, fcrecv_sem, rsend_sem, rrecv_sem,
):
    rows, width = x_ref.shape
    clusters = CLUS_OWN * n
    me = lax.axis_index("owner").astype(jnp.int32)
    other = 1 - lax.axis_index("tile").astype(jnp.int32)

    barrier = pltpu.get_barrier_semaphore()

    def greet(q, carry):
        pl.semaphore_signal(
            barrier, inc=1, device_id={"owner": flipped(me, q, n)}, device_id_type=MESH
        )
        return carry

    lax.fori_loop(1, n, greet, 0)
    pl.semaphore_signal(barrier, inc=1, device_id={"tile": other}, device_id_type=MESH)

    def rows_copy(q):
        return pltpu.make_async_remote_copy(
            src_ref=outgoing.at[q], dst_ref=held.at[0, q],
            send_sem=send_sem.at[q], recv_sem=recv_sem.at[q],
            device_id={"owner": flipped(me, q, n)}, device_id_type=MESH,
        )

    def count_copy(q):
        return pltpu.make_async_remote_copy(
            src_ref=count_out.at[q], dst_ref=count_in.at[0, q],
            send_sem=csend_sem.at[q], recv_sem=crecv_sem.at[q],
            device_id={"owner": flipped(me, q, n)}, device_id_type=MESH,
        )

    def rows_forward(q):
        return pltpu.make_async_remote_copy(
            src_ref=held.at[0, q], dst_ref=held.at[1, q],
            send_sem=fsend_sem.at[q], recv_sem=frecv_sem.at[q],
            device_id={"tile": other}, device_id_type=MESH,
        )

    def count_forward(q):
        return pltpu.make_async_remote_copy(
            src_ref=count_in.at[0, q], dst_ref=count_in.at[1, q],
            send_sem=fcsend_sem.at[q], recv_sem=fcrecv_sem.at[q],
            device_id={"tile": other}, device_id_type=MESH,
        )

    def score_copy(q):
        return pltpu.make_async_remote_copy(
            src_ref=score_out.at[q], dst_ref=score_in.at[q],
            send_sem=rsend_sem.at[q], recv_sem=rrecv_sem.at[q],
            device_id={"owner": flipped(me, q, n)}, device_id_type=MESH,
        )

    piece = 128

    def normalise(step, carry):
        at = pl.ds(pl.multiple_of(step * piece, piece), piece)
        values = x_ref[at, :].astype(jnp.float32)
        scale = lax.rsqrt(jnp.sum(values * values, axis=1, keepdims=True) + epsilon)
        unit[at, :] = (values * scale).astype(jnp.bfloat16)
        return carry

    lax.fori_loop(0, rows // piece, normalise, 0)

    ids = id_ref[...]
    member = lax.broadcasted_iota(jnp.int32, (clusters, rows), 0) == ids
    onehot = jnp.where(member, 1.0, 0.0)
    ranks = jnp.zeros((clusters, rows), jnp.float32)
    for first in range(0, rows, piece):
        earlier = (
            lax.broadcasted_iota(jnp.int32, (piece, rows), 0) + first
            < lax.broadcasted_iota(jnp.int32, (piece, rows), 1)
        )
        ranks += jnp.dot(
            onehot[:, first : first + piece].astype(jnp.bfloat16),
            jnp.where(earlier, 1.0, 0.0).astype(jnp.bfloat16),
            preferred_element_type=jnp.float32,
        )
    within_ref[...] = jnp.sum(onehot * ranks, axis=0, keepdims=True)

    def pack(q, rows_ref, counts_ref):
        target = CLUS_OWN * flipped(me, q, n)
        within = within_ref[...]
        slots = lax.broadcasted_iota(jnp.int32, (cap, rows), 0).astype(jnp.float32)
        picks = []
        for c in range(CLUS_OWN):
            here = id_ref[...] == target + c
            key = jnp.where(here, within, -1.0)
            picks.append(jnp.where(slots == key, 1.0, 0.0).astype(jnp.bfloat16))
            count = jnp.sum(jnp.where(here, 1.0, 0.0), axis=1, keepdims=True)
            counts_ref[c : c + 1, :] = jnp.broadcast_to(count, (1, LANES))
        pick = jnp.concatenate(picks, axis=0)
        rows_ref[...] = jnp.dot(
            pick, unit[...], preferred_element_type=jnp.float32
        ).astype(jnp.bfloat16)

    def clear(q, carry):
        count_out[q] = jnp.zeros((8, LANES), jnp.float32)
        score_out[q] = jnp.zeros((8, LANES), jnp.float32)
        for c in range(CLUS_OWN):
            sums[q, c] = jnp.zeros((8, cap), jnp.float32)
        return carry

    lax.fori_loop(0, n, clear, 0)
    score_in[0] = jnp.zeros((8, LANES), jnp.float32)
    count_in[0, 0] = jnp.zeros((8, LANES), jnp.float32)
    pl.semaphore_wait(barrier, n)

    def send(q, carry):
        pack(q, outgoing.at[q], count_out.at[q])
        rows_copy(q).start()
        count_copy(q).start()
        return carry

    lax.fori_loop(n // 2, n, send, 0)
    lax.fori_loop(1, n // 2, send, 0)
    pack(0, held.at[0, 0], count_in.at[0, 0])

    def block(u, a, c):
        return held[u, a, c * cap : (c + 1) * cap, :]

    def add_pair(u, b, a, c):
        cosine = lax.dot_general(
            block(u, b, c), block(0, a, c), (((1,), (1,)), ((), ())),
            preferred_element_type=jnp.float32,
        )
        live = lax.broadcasted_iota(jnp.int32, (cap, cap), 0).astype(jnp.float32) < (
            count_in[u, b, c : c + 1, 0:cap]
        )
        shift = jnp.where(live, -sharpness, -1e30)
        return fold(jnp.exp(cosine * sharpness + shift))

    def work(k):
        rows_forward(k).start()
        count_forward(k).start()

        def early(a, carry):
            new = []
            for c in range(CLUS_OWN):
                sums[a, c] += add_pair(0, k, a, c)
                new.append(carry[c] + add_pair(0, a, k, c) + add_pair(1, a, k, c))
            return tuple(new)

        mine = lax.fori_loop(
            0, k, early, tuple(jnp.zeros((8, cap), jnp.float32) for _ in range(CLUS_OWN))
        )
        for c in range(CLUS_OWN):
            sums[k, c] += mine[c] + add_pair(0, k, k, c)
        rows_forward(k).wait_recv()
        count_forward(k).wait_recv()

        def late(a, carry):
            for c in range(CLUS_OWN):
                sums[a, c] += add_pair(1, k, a, c)
            return carry

        lax.fori_loop(0, k + 1, late, 0)

    work(0)
    spread[...] = jnp.where(
        lax.broadcasted_iota(jnp.int32, (LANES, rows), 0).astype(jnp.float32) == within_ref[...],
        1.0, 0.0,
    )

    def arrive(k, carry):
        rows_copy(k).wait_recv()
        count_copy(k).wait_recv()
        work(k)
        return carry

    lax.fori_loop(1, n, arrive, 0)

    def give_back(q, carry):
        for c in range(CLUS_OWN):
            score_out[q, c : c + 1, 0:cap] = jnp.sum(sums[q, c], axis=0, keepdims=True)
        score_copy(q).start()
        return carry

    lax.fori_loop(1, n, give_back, 0)
    for c in range(CLUS_OWN):
        score_in[0, c : c + 1, 0:cap] = jnp.sum(sums[0, c], axis=0, keepdims=True)

    def finish(q, carry):
        rows_copy(q).wait_send()
        count_copy(q).wait_send()
        return carry

    lax.fori_loop(1, n, finish, 0)

    def finish_forward(q, carry):
        rows_forward(q).wait_send()
        count_forward(q).wait_send()
        return carry

    lax.fori_loop(0, n, finish_forward, 0)

    def collect(q, carry):
        score_copy(q).wait()
        return carry

    lax.fori_loop(1, n, collect, 0)

    chosen[...] = jnp.dot(
        score_in[...].reshape(n * 8, LANES), spread[...],
        preferred_element_type=jnp.float32, precision=lax.Precision.HIGHEST,
    ).reshape(n, 8, rows)

    def choose(q, total):
        target = CLUS_OWN * flipped(me, q, n)
        for c in range(CLUS_OWN):
            total = total + jnp.where(id_ref[...] == target + c, chosen[q, c : c + 1, :], 0.0)
        return total

    score = lax.fori_loop(0, n, choose, jnp.zeros((1, rows), jnp.float32))
    out_ref[...] = jnp.log(score)


def shards(embeddings, cluster_ids):
    n = lax.axis_size("owner")
    rows, width = embeddings.shape
    cap = 2 * rows // (CLUS_OWN * n)
    dma = pltpu.SemaphoreType.DMA
    result = pl.pallas_call(
        functools.partial(dup_kernel, n, cap),
        out_shape=jax.ShapeDtypeStruct((1, rows), jnp.float32),
        in_specs=[pl.BlockSpec(memory_space=pltpu.VMEM)] * 2,
        out_specs=pl.BlockSpec(memory_space=pltpu.VMEM),
        scratch_shapes=[
            pltpu.VMEM((rows, width), jnp.bfloat16),
            pltpu.VMEM((1, rows), jnp.float32),
            pltpu.VMEM((n, 8, rows), jnp.float32),
            pltpu.VMEM((n, CLUS_OWN * cap, width), jnp.bfloat16),
            pltpu.VMEM((2, n, CLUS_OWN * cap, width), jnp.bfloat16),
            pltpu.VMEM((n, 8, LANES), jnp.float32),
            pltpu.VMEM((2, n, 8, LANES), jnp.float32),
            pltpu.VMEM((n, CLUS_OWN, 8, cap), jnp.float32),
            pltpu.VMEM((n, 8, LANES), jnp.float32),
            pltpu.VMEM((n, 8, LANES), jnp.float32),
            pltpu.VMEM((LANES, rows), jnp.float32),
        ] + [dma((n,))] * 10,
        compiler_params=pltpu.CompilerParams(
            collective_id=0, has_side_effects=True, vmem_limit_bytes=48 * 1024 * 1024
        ),
    )(embeddings, cluster_ids.reshape(1, rows))
    return result.reshape(rows)


def solution(mesh):
    placed = (P(("groups", "owner", "tile"), None), P(("groups", "owner", "tile")))
    return jax.shard_map(
        shards,
        mesh=mesh,
        in_specs=placed,
        out_specs=P(("groups", "owner", "tile")),
        check_vma=False,
    )
```

```python
import functools

import jax
import jax.numpy as jnp
from jax import lax
from jax.experimental import pallas as pl
from jax.experimental.pallas import tpu as pltpu
from jax.sharding import PartitionSpec as P

CLUS_OWN = 2
LANES = 128
MESH = pl.DeviceIdType.MESH

epsilon = 1e-06
sharpness = 20.0


def flipped(index, offset, count):
    total = 0
    bit = 1
    while bit < count:
        digit = lax.rem(lax.div(index, bit) + lax.div(offset, bit), 2)
        total = total + digit * bit
        bit *= 2
    return total


def fold(values):
    rows, lanes = values.shape
    return jnp.sum(values.reshape(rows // 8, 8, lanes), axis=0)


def dup_kernel(
    n, cap, x_hbm, id_hbm, out_ref,
    x_ref, id_ref, load_sem, unit, within_ref, chosen, outgoing, held, count_out, count_in, sums,
    score_out, score_in, spread,
    send_sem, recv_sem, csend_sem, crecv_sem,
    fsend_sem, frecv_sem, fcsend_sem, fcrecv_sem, rsend_sem, rrecv_sem,
):
    rows, width = x_ref.shape
    load_ids = pltpu.make_async_copy(id_hbm, id_ref, load_sem.at[0])
    load_rows = pltpu.make_async_copy(x_hbm, x_ref, load_sem.at[1])
    load_ids.start()
    load_rows.start()
    clusters = CLUS_OWN * n
    me = lax.axis_index("owner").astype(jnp.int32)
    other = 1 - lax.axis_index("tile").astype(jnp.int32)

    barrier = pltpu.get_barrier_semaphore()

    def greet(q, carry):
        pl.semaphore_signal(
            barrier, inc=1, device_id={"owner": flipped(me, q, n)}, device_id_type=MESH
        )
        return carry

    lax.fori_loop(1, n, greet, 0)
    pl.semaphore_signal(barrier, inc=1, device_id={"tile": other}, device_id_type=MESH)

    def rows_copy(q):
        return pltpu.make_async_remote_copy(
            src_ref=outgoing.at[q], dst_ref=held.at[0, q],
            send_sem=send_sem.at[q], recv_sem=recv_sem.at[q],
            device_id={"owner": flipped(me, q, n)}, device_id_type=MESH,
        )

    def count_copy(q):
        return pltpu.make_async_remote_copy(
            src_ref=count_out.at[q], dst_ref=count_in.at[0, q],
            send_sem=csend_sem.at[q], recv_sem=crecv_sem.at[q],
            device_id={"owner": flipped(me, q, n)}, device_id_type=MESH,
        )

    def rows_forward(q):
        return pltpu.make_async_remote_copy(
            src_ref=held.at[0, q], dst_ref=held.at[1, q],
            send_sem=fsend_sem.at[q], recv_sem=frecv_sem.at[q],
            device_id={"tile": other}, device_id_type=MESH,
        )

    def count_forward(q):
        return pltpu.make_async_remote_copy(
            src_ref=count_in.at[0, q], dst_ref=count_in.at[1, q],
            send_sem=fcsend_sem.at[q], recv_sem=fcrecv_sem.at[q],
            device_id={"tile": other}, device_id_type=MESH,
        )

    def score_copy(q):
        return pltpu.make_async_remote_copy(
            src_ref=score_out.at[q], dst_ref=score_in.at[q],
            send_sem=rsend_sem.at[q], recv_sem=rrecv_sem.at[q],
            device_id={"owner": flipped(me, q, n)}, device_id_type=MESH,
        )

    load_ids.wait()
    ids = id_ref[...]
    member = lax.broadcasted_iota(jnp.int32, (clusters, rows), 0) == ids
    onehot = jnp.where(member, 1.0, 0.0)
    piece = 128
    ranks = jnp.zeros((clusters, rows), jnp.float32)
    for first in range(0, rows, piece):
        earlier = (
            lax.broadcasted_iota(jnp.int32, (piece, rows), 0) + first
            < lax.broadcasted_iota(jnp.int32, (piece, rows), 1)
        )
        ranks += jnp.dot(
            onehot[:, first : first + piece].astype(jnp.bfloat16),
            jnp.where(earlier, 1.0, 0.0).astype(jnp.bfloat16),
            preferred_element_type=jnp.float32,
        )
    within_ref[...] = jnp.sum(onehot * ranks, axis=0, keepdims=True)

    def normalise(step, carry):
        at = pl.ds(pl.multiple_of(step * piece, piece), piece)
        values = x_ref[at, :].astype(jnp.float32)
        scale = lax.rsqrt(jnp.sum(values * values, axis=1, keepdims=True) + epsilon)
        unit[at, :] = (values * scale).astype(jnp.bfloat16)
        return carry

    load_rows.wait()
    lax.fori_loop(0, rows // piece, normalise, 0)

    def pack(q, rows_ref, counts_ref):
        target = CLUS_OWN * flipped(me, q, n)
        within = within_ref[...]
        slots = lax.broadcasted_iota(jnp.int32, (cap, rows), 0).astype(jnp.float32)
        picks = []
        for c in range(CLUS_OWN):
            here = id_ref[...] == target + c
            key = jnp.where(here, within, -1.0)
            picks.append(jnp.where(slots == key, 1.0, 0.0).astype(jnp.bfloat16))
            count = jnp.sum(jnp.where(here, 1.0, 0.0), axis=1, keepdims=True)
            counts_ref[c : c + 1, :] = jnp.broadcast_to(count, (1, LANES))
        pick = jnp.concatenate(picks, axis=0)
        rows_ref[...] = jnp.dot(
            pick, unit[...], preferred_element_type=jnp.float32
        ).astype(jnp.bfloat16)

    def clear(q, carry):
        count_out[q] = jnp.zeros((8, LANES), jnp.float32)
        score_out[q] = jnp.zeros((8, LANES), jnp.float32)
        for c in range(CLUS_OWN):
            sums[q, c] = jnp.zeros((8, cap), jnp.float32)
        return carry

    lax.fori_loop(0, n, clear, 0)
    score_in[0] = jnp.zeros((8, LANES), jnp.float32)
    count_in[0, 0] = jnp.zeros((8, LANES), jnp.float32)
    pack(n // 2, outgoing.at[n // 2], count_out.at[n // 2])
    pl.semaphore_wait(barrier, n)

    def send(q, carry):
        pack(q, outgoing.at[q], count_out.at[q])
        rows_copy(q).start()
        count_copy(q).start()
        return carry

    def paced(q, carry):
        pack(q, outgoing.at[q], count_out.at[q])
        rows_copy(q - 2).wait_send()
        rows_copy(q).start()
        count_copy(q).start()
        return carry
    rows_copy(n // 2).start()
    count_copy(n // 2).start()
    lax.fori_loop(n // 2 + 1, n // 2 + 2, send, 0)
    lax.fori_loop(1, n // 2, send, 0)
    lax.fori_loop(n // 2 + 2, n, paced, 0)
    pack(0, held.at[0, 0], count_in.at[0, 0])

    def both(a, c):
        return jnp.concatenate([block(0, a, c), block(1, a, c)], axis=0)

    def block(u, a, c):
        return held[u, a, c * cap : (c + 1) * cap, :]

    def add_pair(b, a, c):
        cosine = lax.dot_general(
            both(b, c), block(0, a, c), (((1,), (1,)), ((), ())),
            preferred_element_type=jnp.float32,
        )
        slot = lax.broadcasted_iota(jnp.int32, (cap, cap), 0).astype(jnp.float32)
        total = jnp.zeros((8, cap), jnp.float32)
        for u in range(2):
            live = slot < count_in[u, b, c : c + 1, 0:cap]
            shift = jnp.where(live, -sharpness, -1e30)
            total += fold(jnp.exp(cosine[u * cap : (u + 1) * cap] * sharpness + shift))
        return total

    def work(k):
        rows_forward(k).start()
        count_forward(k).start()

        def early(a, carry):
            new = []
            for c in range(CLUS_OWN):
                new.append(carry[c] + add_pair(a, k, c))
            return tuple(new)

        mine = lax.fori_loop(
            0, k, early, tuple(jnp.zeros((8, cap), jnp.float32) for _ in range(CLUS_OWN))
        )
        for c in range(CLUS_OWN):
            sums[k, c] = mine[c]
        rows_forward(k).wait_recv()
        count_forward(k).wait_recv()

        def late(a, carry):
            for c in range(CLUS_OWN):
                sums[a, c] += add_pair(k, a, c)
            return carry

        lax.fori_loop(0, k + 1, late, 0)

    def wide(first, last, c):
        at = slice(c * cap, (c + 1) * cap)
        return held[0, first:last, at, :].reshape((last - first) * cap, width)

    def kernels(left, right, lives):
        cosine = lax.dot_general(
            left, right, (((1,), (1,)), ((), ())), preferred_element_type=jnp.float32
        )
        lanes = right.shape[0]
        slot = lax.broadcasted_iota(jnp.int32, (cap, cap), 0).astype(jnp.float32)
        parts = []
        shifts = [jnp.where(slot < live[:, 0:cap], -sharpness, -1e30) for live in lives]
        for lane in range(0, lanes, cap):
            total = jnp.zeros((8, cap), jnp.float32)
            for b, shift in enumerate(shifts):
                piece_cos = cosine[b * cap : (b + 1) * cap, lane : lane + cap]
                total += fold(jnp.exp(piece_cos * sharpness + shift))
            parts.append(total)
        return parts

    def work_fixed(k):
        rows_forward(k).start()
        count_forward(k).start()
        for c in range(CLUS_OWN):
            total = jnp.zeros((8, cap), jnp.float32)
            for b in range(k):
                lives = [count_in[u, b, c : c + 1, :] for u in range(2)]
                total += kernels(both(b, c), block(0, k, c), lives)[0]
            sums[k, c] = total
        rows_forward(k).wait_recv()
        count_forward(k).wait_recv()
        for c in range(CLUS_OWN):
            lives = [count_in[u, k, c : c + 1, :] for u in range(2)]
            for a in range(0, k + 1, 2):
                last = min(a + 2, k + 1)
                parts = kernels(both(k, c), wide(a, last, c), lives)
                for i in range(last - a):
                    sums[a + i, c] += parts[i]

    work(0)
    spread[...] = jnp.where(
        lax.broadcasted_iota(jnp.int32, (LANES, rows), 0).astype(jnp.float32) == within_ref[...],
        1.0, 0.0,
    )

    def arrive(k, carry):
        rows_copy(k).wait_recv()
        count_copy(k).wait_recv()
        work(k)
        return carry

    if n <= 8:
        for k in range(1, n):
            rows_copy(k).wait_recv()
            count_copy(k).wait_recv()
            work_fixed(k)
    else:
        lax.fori_loop(1, n, arrive, 0)

    def give_back(q, carry):
        for c in range(CLUS_OWN):
            score_out[q, c : c + 1, 0:cap] = jnp.sum(sums[q, c], axis=0, keepdims=True)
        score_copy(q).start()
        return carry

    lax.fori_loop(1, n, give_back, 0)
    for c in range(CLUS_OWN):
        score_in[0, c : c + 1, 0:cap] = jnp.sum(sums[0, c], axis=0, keepdims=True)

    def finish(q, carry):
        count_copy(q).wait_send()
        return carry

    def finish_rows(q, carry):
        rows_copy(q).wait_send()
        return carry

    lax.fori_loop(1, n // 2, finish_rows, 0)
    lax.fori_loop(n - 2, n, finish_rows, 0)
    lax.fori_loop(1, n, finish, 0)

    def finish_forward(q, carry):
        rows_forward(q).wait_send()
        count_forward(q).wait_send()
        return carry

    lax.fori_loop(0, n, finish_forward, 0)

    def collect(q, carry):
        score_copy(q).wait()
        return carry

    lax.fori_loop(1, n, collect, 0)

    chosen[...] = jnp.dot(
        score_in[...].reshape(n * 8, LANES), spread[...],
        preferred_element_type=jnp.float32, precision=lax.Precision.HIGHEST,
    ).reshape(n, 8, rows)

    def choose(q, total):
        target = CLUS_OWN * flipped(me, q, n)
        for c in range(CLUS_OWN):
            total = total + jnp.where(id_ref[...] == target + c, chosen[q, c : c + 1, :], 0.0)
        return total

    score = lax.fori_loop(0, n, choose, jnp.zeros((1, rows), jnp.float32))
    out_ref[...] = jnp.log(score)


def shards(embeddings, cluster_ids):
    n = lax.axis_size("owner")
    rows, width = embeddings.shape
    cap = 2 * rows // (CLUS_OWN * n)
    dma = pltpu.SemaphoreType.DMA
    result = pl.pallas_call(
        functools.partial(dup_kernel, n, cap),
        out_shape=jax.ShapeDtypeStruct((1, rows), jnp.float32),
        in_specs=[pl.BlockSpec(memory_space=pl.ANY)] * 2,
        out_specs=pl.BlockSpec(memory_space=pltpu.VMEM),
        scratch_shapes=[
            pltpu.VMEM((rows, width), jnp.bfloat16),
            pltpu.VMEM((1, rows), jnp.int32),
            dma((2,)),
            pltpu.VMEM((rows, width), jnp.bfloat16),
            pltpu.VMEM((1, rows), jnp.float32),
            pltpu.VMEM((n, 8, rows), jnp.float32),
            pltpu.VMEM((n, CLUS_OWN * cap, width), jnp.bfloat16),
            pltpu.VMEM((2, n, CLUS_OWN * cap, width), jnp.bfloat16),
            pltpu.VMEM((n, 8, LANES), jnp.float32),
            pltpu.VMEM((2, n, 8, LANES), jnp.float32),
            pltpu.VMEM((n, CLUS_OWN, 8, cap), jnp.float32),
            pltpu.VMEM((n, 8, LANES), jnp.float32),
            pltpu.VMEM((n, 8, LANES), jnp.float32),
            pltpu.VMEM((LANES, rows), jnp.float32),
        ] + [dma((n,))] * 10,
        compiler_params=pltpu.CompilerParams(
            collective_id=0, has_side_effects=True, vmem_limit_bytes=48 * 1024 * 1024
        ),
    )(embeddings, cluster_ids.reshape(1, rows))
    return result.reshape(rows)


def solution(mesh):
    placed = (P(("groups", "owner", "tile"), None), P(("groups", "owner", "tile")))
    return jax.shard_map(
        shards,
        mesh=mesh,
        in_specs=placed,
        out_specs=P(("groups", "owner", "tile")),
        check_vma=False,
    )
```

```python
import functools

import jax
import jax.numpy as jnp
from jax import lax
from jax.experimental import pallas as pl
from jax.experimental.pallas import tpu as pltpu
from jax.sharding import PartitionSpec as P

CLUS_OWN = 2
LANES = 128
MESH = pl.DeviceIdType.MESH

epsilon = 1e-06
sharpness = 20.0


def flipped(index, offset, count):
    far = count // 2
    offset = jnp.where(offset < far, offset, offset + 1 - 2 * lax.rem(offset, 2))
    total = 0
    bit = 1
    while bit < count:
        digit = lax.rem(lax.div(index, bit) + lax.div(offset, bit), 2)
        total = total + digit * bit
        bit *= 2
    return total


def fold(values):
    rows, lanes = values.shape
    return jnp.sum(values.reshape(rows // 8, 8, lanes), axis=0)


def dup_kernel(
    n, cap, x_hbm, id_hbm, out_ref,
    x_ref, id_ref, load_sem, unit, within_ref, chosen, outgoing, held, count_out, count_in, sums,
    score_out, score_in, spread,
    send_sem, recv_sem, csend_sem, crecv_sem,
    fsend_sem, frecv_sem, fcsend_sem, fcrecv_sem, rsend_sem, rrecv_sem,
):
    rows, width = x_ref.shape
    load_ids = pltpu.make_async_copy(id_hbm, id_ref, load_sem.at[0])
    load_rows = pltpu.make_async_copy(x_hbm, x_ref, load_sem.at[1])
    load_ids.start()
    load_rows.start()
    clusters = CLUS_OWN * n
    me = lax.axis_index("owner").astype(jnp.int32)
    other = 1 - lax.axis_index("tile").astype(jnp.int32)

    barrier = pltpu.get_barrier_semaphore()

    def greet(q, carry):
        pl.semaphore_signal(
            barrier, inc=1, device_id={"owner": flipped(me, q, n)}, device_id_type=MESH
        )
        return carry

    lax.fori_loop(1, n, greet, 0)
    pl.semaphore_signal(barrier, inc=1, device_id={"tile": other}, device_id_type=MESH)

    def rows_copy(q):
        return pltpu.make_async_remote_copy(
            src_ref=outgoing.at[q], dst_ref=held.at[0, q],
            send_sem=send_sem.at[q], recv_sem=recv_sem.at[q],
            device_id={"owner": flipped(me, q, n)}, device_id_type=MESH,
        )

    def count_copy(q):
        return pltpu.make_async_remote_copy(
            src_ref=count_out.at[q], dst_ref=count_in.at[0, q],
            send_sem=csend_sem.at[q], recv_sem=crecv_sem.at[q],
            device_id={"owner": flipped(me, q, n)}, device_id_type=MESH,
        )

    def rows_forward(q):
        return pltpu.make_async_remote_copy(
            src_ref=held.at[0, q], dst_ref=held.at[1, q],
            send_sem=fsend_sem.at[q], recv_sem=frecv_sem.at[q],
            device_id={"tile": other}, device_id_type=MESH,
        )

    def count_forward(q):
        return pltpu.make_async_remote_copy(
            src_ref=count_in.at[0, q], dst_ref=count_in.at[1, q],
            send_sem=fcsend_sem.at[q], recv_sem=fcrecv_sem.at[q],
            device_id={"tile": other}, device_id_type=MESH,
        )

    def score_copy(q):
        return pltpu.make_async_remote_copy(
            src_ref=score_out.at[q], dst_ref=score_in.at[q],
            send_sem=rsend_sem.at[q], recv_sem=rrecv_sem.at[q],
            device_id={"owner": flipped(me, q, n)}, device_id_type=MESH,
        )

    load_ids.wait()
    ids = id_ref[...]
    member = lax.broadcasted_iota(jnp.int32, (clusters, rows), 0) == ids
    onehot = jnp.where(member, 1.0, 0.0)
    piece = 128
    ranks = jnp.zeros((clusters, rows), jnp.float32)
    for first in range(0, rows, piece):
        earlier = (
            lax.broadcasted_iota(jnp.int32, (piece, rows), 0) + first
            < lax.broadcasted_iota(jnp.int32, (piece, rows), 1)
        )
        ranks += jnp.dot(
            onehot[:, first : first + piece].astype(jnp.bfloat16),
            jnp.where(earlier, 1.0, 0.0).astype(jnp.bfloat16),
            preferred_element_type=jnp.float32,
        )
    within_ref[...] = jnp.sum(onehot * ranks, axis=0, keepdims=True)

    def normalise(step, carry):
        at = pl.ds(pl.multiple_of(step * piece, piece), piece)
        values = x_ref[at, :].astype(jnp.float32)
        scale = lax.rsqrt(jnp.sum(values * values, axis=1, keepdims=True) + epsilon)
        unit[at, :] = (values * scale).astype(jnp.bfloat16)
        return carry

    load_rows.wait()
    lax.fori_loop(0, rows // piece, normalise, 0)

    def pack(q, rows_ref, counts_ref):
        target = CLUS_OWN * flipped(me, q, n)
        within = within_ref[...]
        slots = lax.broadcasted_iota(jnp.int32, (cap, rows), 0).astype(jnp.float32)
        picks = []
        for c in range(CLUS_OWN):
            here = id_ref[...] == target + c
            key = jnp.where(here, within, -1.0)
            picks.append(jnp.where(slots == key, 1.0, 0.0).astype(jnp.bfloat16))
            count = jnp.sum(jnp.where(here, 1.0, 0.0), axis=1, keepdims=True)
            counts_ref[c : c + 1, :] = jnp.broadcast_to(count, (1, LANES))
        pick = jnp.concatenate(picks, axis=0)
        rows_ref[...] = jnp.dot(
            pick, unit[...], preferred_element_type=jnp.float32
        ).astype(jnp.bfloat16)

    def clear(q, carry):
        count_out[q] = jnp.zeros((8, LANES), jnp.float32)
        score_out[q] = jnp.zeros((8, LANES), jnp.float32)
        for c in range(CLUS_OWN):
            sums[q, c] = jnp.zeros((8, cap), jnp.float32)
        return carry

    lax.fori_loop(0, n, clear, 0)
    score_in[0] = jnp.zeros((8, LANES), jnp.float32)
    count_in[0, 0] = jnp.zeros((8, LANES), jnp.float32)
    pack(n // 2, outgoing.at[n // 2], count_out.at[n // 2])
    pl.semaphore_wait(barrier, n)

    def send(q, carry):
        pack(q, outgoing.at[q], count_out.at[q])
        rows_copy(q).start()
        count_copy(q).start()
        return carry

    def paced(q, carry):
        pack(q, outgoing.at[q], count_out.at[q])
        rows_copy(q - 2).wait_send()
        rows_copy(q).start()
        count_copy(q).start()
        return carry
    rows_copy(n // 2).start()
    count_copy(n // 2).start()
    lax.fori_loop(n // 2 + 1, n // 2 + 2, send, 0)
    lax.fori_loop(1, n // 2, send, 0)
    lax.fori_loop(n // 2 + 2, n, paced, 0)
    pack(0, held.at[0, 0], count_in.at[0, 0])

    def both(a, c):
        return jnp.concatenate([block(0, a, c), block(1, a, c)], axis=0)

    def block(u, a, c):
        return held[u, a, c * cap : (c + 1) * cap, :]

    def add_pair(b, a, c):
        cosine = lax.dot_general(
            both(b, c), block(0, a, c), (((1,), (1,)), ((), ())),
            preferred_element_type=jnp.float32,
        )
        slot = lax.broadcasted_iota(jnp.int32, (cap, cap), 0).astype(jnp.float32)
        total = jnp.zeros((8, cap), jnp.float32)
        for u in range(2):
            live = slot < count_in[u, b, c : c + 1, 0:cap]
            shift = jnp.where(live, -sharpness, -1e30)
            total += fold(jnp.exp(cosine[u * cap : (u + 1) * cap] * sharpness + shift))
        return total

    def work(k):
        rows_forward(k).start()
        count_forward(k).start()

        def early(a, carry):
            new = []
            for c in range(CLUS_OWN):
                new.append(carry[c] + add_pair(a, k, c))
            return tuple(new)

        mine = lax.fori_loop(
            0, k, early, tuple(jnp.zeros((8, cap), jnp.float32) for _ in range(CLUS_OWN))
        )
        for c in range(CLUS_OWN):
            sums[k, c] = mine[c]
        rows_forward(k).wait_recv()
        count_forward(k).wait_recv()

        def late(a, carry):
            for c in range(CLUS_OWN):
                sums[a, c] += add_pair(k, a, c)
            return carry

        lax.fori_loop(0, k + 1, late, 0)

    def wide(first, last, c):
        at = slice(c * cap, (c + 1) * cap)
        return held[0, first:last, at, :].reshape((last - first) * cap, width)

    def kernels(left, right, lives):
        cosine = lax.dot_general(
            left, right, (((1,), (1,)), ((), ())), preferred_element_type=jnp.float32
        )
        lanes = right.shape[0]
        slot = lax.broadcasted_iota(jnp.int32, (cap, cap), 0).astype(jnp.float32)
        parts = []
        shifts = [jnp.where(slot < live[:, 0:cap], -sharpness, -1e30) for live in lives]
        for lane in range(0, lanes, cap):
            total = jnp.zeros((8, cap), jnp.float32)
            for b, shift in enumerate(shifts):
                piece_cos = cosine[b * cap : (b + 1) * cap, lane : lane + cap]
                total += fold(jnp.exp(piece_cos * sharpness + shift))
            parts.append(total)
        return parts

    def work_fixed(k):
        rows_forward(k).start()
        count_forward(k).start()
        for c in range(CLUS_OWN):
            total = jnp.zeros((8, cap), jnp.float32)
            for b in range(k):
                lives = [count_in[u, b, c : c + 1, :] for u in range(2)]
                total += kernels(both(b, c), block(0, k, c), lives)[0]
            sums[k, c] = total
        rows_forward(k).wait_recv()
        count_forward(k).wait_recv()
        for c in range(CLUS_OWN):
            lives = [count_in[u, k, c : c + 1, :] for u in range(2)]
            for a in range(0, k + 1, 2):
                last = min(a + 2, k + 1)
                parts = kernels(both(k, c), wide(a, last, c), lives)
                for i in range(last - a):
                    sums[a + i, c] += parts[i]

    work(0)
    spread[...] = jnp.where(
        lax.broadcasted_iota(jnp.int32, (LANES, rows), 0).astype(jnp.float32) == within_ref[...],
        1.0, 0.0,
    )

    def arrive(k, carry):
        rows_copy(k).wait_recv()
        count_copy(k).wait_recv()
        work(k)
        return carry

    if n <= 8:
        for k in range(1, n):
            rows_copy(k).wait_recv()
            count_copy(k).wait_recv()
            work_fixed(k)
    else:
        lax.fori_loop(1, n, arrive, 0)

    def give_back(q, carry):
        for c in range(CLUS_OWN):
            score_out[q, c : c + 1, 0:cap] = jnp.sum(sums[q, c], axis=0, keepdims=True)
        score_copy(q).start()
        return carry

    lax.fori_loop(1, n, give_back, 0)
    for c in range(CLUS_OWN):
        score_in[0, c : c + 1, 0:cap] = jnp.sum(sums[0, c], axis=0, keepdims=True)

    def finish(q, carry):
        count_copy(q).wait_send()
        return carry

    def finish_rows(q, carry):
        rows_copy(q).wait_send()
        return carry

    lax.fori_loop(1, n // 2, finish_rows, 0)
    lax.fori_loop(n - 2, n, finish_rows, 0)
    lax.fori_loop(1, n, finish, 0)

    def finish_forward(q, carry):
        rows_forward(q).wait_send()
        count_forward(q).wait_send()
        return carry

    lax.fori_loop(0, n, finish_forward, 0)

    def collect(q, carry):
        score_copy(q).wait()
        return carry

    lax.fori_loop(1, n, collect, 0)

    chosen[...] = jnp.dot(
        score_in[...].reshape(n * 8, LANES), spread[...],
        preferred_element_type=jnp.float32, precision=lax.Precision.HIGHEST,
    ).reshape(n, 8, rows)

    def choose(q, total):
        target = CLUS_OWN * flipped(me, q, n)
        for c in range(CLUS_OWN):
            total = total + jnp.where(id_ref[...] == target + c, chosen[q, c : c + 1, :], 0.0)
        return total

    score = lax.fori_loop(0, n, choose, jnp.zeros((1, rows), jnp.float32))
    out_ref[...] = score


def shards(embeddings, cluster_ids):
    n = lax.axis_size("owner")
    rows, width = embeddings.shape
    cap = 2 * rows // (CLUS_OWN * n)
    dma = pltpu.SemaphoreType.DMA
    result = pl.pallas_call(
        functools.partial(dup_kernel, n, cap),
        out_shape=jax.ShapeDtypeStruct((1, rows), jnp.float32),
        in_specs=[pl.BlockSpec(memory_space=pl.ANY)] * 2,
        out_specs=pl.BlockSpec(memory_space=pltpu.VMEM),
        scratch_shapes=[
            pltpu.VMEM((rows, width), jnp.bfloat16),
            pltpu.VMEM((1, rows), jnp.int32),
            dma((2,)),
            pltpu.VMEM((rows, width), jnp.bfloat16),
            pltpu.VMEM((1, rows), jnp.float32),
            pltpu.VMEM((n, 8, rows), jnp.float32),
            pltpu.VMEM((n, CLUS_OWN * cap, width), jnp.bfloat16),
            pltpu.VMEM((2, n, CLUS_OWN * cap, width), jnp.bfloat16),
            pltpu.VMEM((n, 8, LANES), jnp.float32),
            pltpu.VMEM((2, n, 8, LANES), jnp.float32),
            pltpu.VMEM((n, CLUS_OWN, 8, cap), jnp.float32),
            pltpu.VMEM((n, 8, LANES), jnp.float32),
            pltpu.VMEM((n, 8, LANES), jnp.float32),
            pltpu.VMEM((LANES, rows), jnp.float32),
        ] + [dma((n,))] * 10,
        compiler_params=pltpu.CompilerParams(
            collective_id=0, has_side_effects=True, vmem_limit_bytes=48 * 1024 * 1024
        ),
    )(embeddings, cluster_ids.reshape(1, rows))
    return jnp.log(result.reshape(rows))


def solution(mesh):
    placed = (P(("groups", "owner", "tile"), None), P(("groups", "owner", "tile")))
    return jax.shard_map(
        shards,
        mesh=mesh,
        in_specs=placed,
        out_specs=P(("groups", "owner", "tile")),
        check_vma=False,
    )
```
